32 devices in a mesh: req: 8 (over z, y), head: 4 (over x, core).
Axes of the slice: x: 2, y: 2, z: 4, core: 2. Of those that a mesh axis runs over, the one named last changes fastest.
Arguments:
- tokens: bfloat16 [8192, 1024], P(('req', 'head')), may hold values from -6 to 6
- w_proj: bfloat16 [1024, 2048], P(None, 'head'), may hold values from -0.1875 to 0.1875
- w_out: bfloat16 [1024, 1024], replicated, may hold values from -0.1875 to 0.1875
- kv_cache: bfloat16 [8, 8, 12, 128, 2048], P('req', None, None, None, 'head'), may hold values from -6 to 6
- slot_request: int32 [16], P('req'), may hold values from 0 to 15, each once
- lengths: int32 [16], replicated, may hold values from 1 to 4096
- block_owner: int32 [512, 1], P('req'), may hold values from 0 to 7; in each aligned block of 64 rows (0 to 63, 64 to 127, ...) at most 12 rows name the same one
Outputs:
- mixed: bfloat16 [8192, 1024], P(('req', 'head'))
The draws below stay inside these ranges and needn't reach their ends.
Inputs may be any that keep to these rules, and one draw needn't show every extreme that they name: `block_owner`: within each aligned block of 64 rows no owner appears more than 12 times.
All inputs are finite; a program needn't handle non-finite values.
Results may differ from the reference program's by a relative error of at most 0.0088.
Values may be sent and summed in bfloat16 or wider, within the bound.
A program may use at most 128 MiB of HBM per device.

```python
import math
import jax
import jax.numpy as jnp
import numpy as np
from jax import lax

D = 1024
H = 16
DH = 64
CAND = 512
BLK = 128
MAXB = 32
REQ_DEV = 2
HIST = 4096
REQS = 16
TOKENS = 8192
MOST = 12
N_REQ = 8


def draw_lengths(key, part):
    first, second = jax.random.split(key)
    values = jax.random.randint(first, (REQS,), 1, HIST + 1)
    spot = jax.random.randint(second, (), 0, REQS)
    places = jnp.arange(REQS)
    values = jnp.where(places == spot, HIST, values)
    values = jnp.where(places == (spot + 1) % REQS, 1, values)
    return values.astype(jnp.int32)


def block_levels(own_key, extent, cuts, low, high):
    level = 1.0
    for dim, blocks in cuts:
        draws = jax.random.uniform(jax.random.fold_in(jax.random.fold_in(own_key, 6), dim), (blocks,), jnp.float32, low / len(cuts), high / len(cuts))
        level = level * jnp.repeat(jnp.exp(draws), extent[dim] // blocks).reshape((-1,) + (1,) * (len(extent) - 1 - dim))
    return level


def assign_block(stream_key, own, number, rows, number_of, top, limit, slope):
    order = jax.random.permutation(stream_key, number_of)
    packed, common = shares(number_of, rows * top, limit, slope, True), shares(number_of, rows * top, limit, slope, False)
    places = jnp.arange(number_of)

    def named(sizes, offset_by):
        used = int((sizes > 0).sum())
        fixed = max(1, used // 4)
        moved = fixed + (places - fixed + offset_by * (used - fixed)) % max(1, number_of - fixed)
        return jnp.zeros((number_of,), jnp.int32).at[order[jnp.where(places < fixed, places, moved)]].set(jnp.asarray(sizes, jnp.int32))

    sizes = jnp.where(number % 4 == 0, named(packed, number // 4), named(common, number - number // 4 - 1))
    mixed = jax.random.permutation(jax.random.fold_in(own, 3), number_of)
    source_of, sink = mixed[0:number_of // 2 * 2:2], mixed[1:number_of // 2 * 2:2]
    room = jnp.minimum(sizes[source_of] - 1, limit - sizes[sink]) // 2
    room = jnp.where((source_of == order[0]) | (sink == order[0]) | (sizes[sink] == 0), 0, jnp.maximum(room, 0))
    moved = jax.random.randint(jax.random.fold_in(own, 4), (number_of // 2,), 0, 1 << 20) % (room + 1)
    sizes = sizes.at[source_of].add(-moved).at[sink].add(moved)
    members = jnp.searchsorted(jnp.cumsum(sizes), jnp.arange(rows * top), side="right").astype(jnp.int32)
    listing = members.reshape(top, rows).T
    listing = listing[jax.random.permutation(jax.random.fold_in(own, 1), rows)]
    offset_by = jax.random.randint(jax.random.fold_in(own, 2), (rows, 1), 0, top)
    return jnp.take_along_axis(listing, (jnp.arange(top)[None, :] + offset_by) % top, axis=1)


def shares(amount, total, most, slope, full):
    weights = [(1 << 20) // math.isqrt(rank ** slope) + 1 for rank in range(1, amount + 1)]
    largest = most if full else min(most, max(-(-total // amount), total * weights[0] // sum(weights)))
    least = 1 if total - largest >= amount - 1 else 0
    given, surplus = [largest] + [least] * (amount - 1), total - largest - least * (amount - 1)
    while surplus > 0:
        movable = [i for i in range(1, amount) if given[i] < largest] or [i for i in range(1, amount) if given[i] < most]
        mass, left = sum([weights[i] for i in movable]), surplus
        for i in movable:
            extra = min(most - given[i], max(1, left * weights[i] // mass), surplus)
            given[i] = given[i] + extra
            surplus = surplus - extra
    return np.array(given)


def gaussian(rng, extent, width, limit, shards=(), held_as=jnp.bfloat16):
    drawn = width * jax.random.normal(rng, extent, jnp.float32)
    if shards:
        drawn = drawn * block_levels(rng, extent, shards, -0.22, 0.18)
    return jnp.clip(drawn, -limit, limit).astype(held_as)


def setup_inputs(seed: int = 0) -> dict:
    streams_of = jax.random.split(jax.random.key(seed), 8)
    tokens = gaussian(streams_of[0], (TOKENS, D), 1.0, 6.0, ((0, 32),))
    w_proj = gaussian(streams_of[1], (D, H * 2 * DH), D ** -0.5, 0.1875, ((1, 4),))
    w_out = gaussian(streams_of[2], (H * DH, D), (H * DH) ** -0.5, 0.1875)
    kv_cache = gaussian(streams_of[3], (N_REQ, N_REQ, MOST, BLK, H * 2 * DH), 1.0, 6.0, ((0, 8), (4, 4)))
    slot_request = jax.random.permutation(streams_of[4], REQS).astype(jnp.int32)
    lengths = draw_lengths(jax.random.fold_in(streams_of[7], 71), 0)
    block_owner_keys = jax.random.split(jax.random.fold_in(streams_of[6], 1), (REQS * MAXB) // (REQ_DEV * MAXB))
    block_owner_turns = jax.random.permutation(jax.random.fold_in(streams_of[6], 3), (REQS * MAXB) // (REQ_DEV * MAXB))
    block_owner = jax.vmap(lambda own, number: assign_block(jax.random.fold_in(streams_of[6], 2), own, number, REQ_DEV * MAXB, N_REQ, 1, MOST, 2))(block_owner_keys, block_owner_turns).reshape((REQS * MAXB, 1))
    return dict(tokens=tokens, w_proj=w_proj, w_out=w_out, kv_cache=kv_cache, slot_request=slot_request, lengths=lengths, block_owner=block_owner)


def layer_norm(values):
    mean = lax.optimization_barrier(jnp.mean(values, axis=-1, keepdims=True))
    square = lax.optimization_barrier(jnp.mean(values * values, axis=-1, keepdims=True))
    return (values - mean) * lax.rsqrt(square - mean * mean + 1e-05)

def reference(tokens, w_proj, w_out, kv_cache, slot_request, lengths, block_owner):
    normed = layer_norm(tokens.astype(jnp.float32)).astype(jnp.bfloat16)
    proj = jax.nn.silu(jnp.dot(normed, w_proj, preferred_element_type=jnp.float32))
    proj = proj.reshape(TOKENS, H, 2, DH)
    gate_u = proj[:, :, 0].astype(jnp.bfloat16)
    query = proj[:, :, 1].astype(jnp.bfloat16)
    lens = lengths[slot_request].reshape(N_REQ, REQ_DEV)
    owners = block_owner[:, 0].astype(jnp.int32).reshape(N_REQ, REQ_DEV * MAXB)
    onehot = (owners[:, :, None] == jnp.arange(N_REQ, dtype=jnp.int32)[None, None, :]).astype(jnp.int32)
    rank = lax.optimization_barrier(jnp.sum((jnp.cumsum(onehot, axis=1) - onehot) * onehot, axis=2))
    index = (owners * MOST + rank).astype(jnp.int32)
    query_dev = query.reshape(N_REQ, REQ_DEV, CAND, H, DH)
    scale = 1.0 / DH ** 0.5
    positions = jnp.arange(HIST, dtype=jnp.int32)

    def per_scorer(scorer):
        pool = kv_cache[:, scorer].reshape(N_REQ * MOST, BLK, H * 2 * DH)
        history = pool[index[scorer]].reshape(REQ_DEV, HIST, H, 2, DH)

        def per_request(slot):
            keys = history[slot, :, :, 0].astype(jnp.float32)
            values = history[slot, :, :, 1].astype(jnp.float32)
            scores = jnp.einsum('chd,phd->hcp', query_dev[scorer, slot].astype(jnp.float32), keys) * scale
            live = positions < lens[scorer, slot]
            weights = jnp.where(live[None, None, :], jax.nn.silu(scores), 0.0).astype(jnp.bfloat16)
            weights = lax.optimization_barrier(weights).astype(jnp.float32)
            return jnp.einsum('hcp,phd->chd', weights, values)
        return lax.map(per_request, jnp.arange(REQ_DEV, dtype=jnp.int32))
    attn = lax.map(per_scorer, jnp.arange(N_REQ, dtype=jnp.int32))
    attn = attn.reshape(TOKENS, H * DH).astype(jnp.bfloat16)
    hidden = layer_norm(attn.astype(jnp.float32)) * gate_u.reshape(TOKENS, H * DH).astype(jnp.float32)
    hidden = hidden.astype(jnp.bfloat16)
    return jnp.dot(hidden, w_out, preferred_element_type=jnp.float32).astype(jnp.bfloat16)
```

```python
import functools

import jax
import jax.numpy as jnp
from jax import lax
from jax.experimental import pallas as pl
from jax.experimental.pallas import tpu as pltpu
from jax.sharding import PartitionSpec as P

DH = 64
CAND = 512
BLK = 128
MAXB = 32
LANES = 2 * DH


def proj_kernel(x_ref, w_ref, gate_ref, query_ref):
    x = x_ref[...].astype(jnp.float32)
    mean = jnp.mean(x, axis=-1, keepdims=True)
    square = jnp.mean(x * x, axis=-1, keepdims=True)
    normed = ((x - mean) * lax.rsqrt(square - mean * mean + 1e-05)).astype(jnp.bfloat16)
    half = 0.5 * jnp.dot(normed, w_ref[...], preferred_element_type=jnp.float32)
    out = half + half * jnp.tanh(half)
    first = lax.broadcasted_iota(jnp.int32, (x.shape[0], LANES), 1) < DH
    for pair in range(w_ref.shape[1] // (2 * LANES)):
        even = out[:, 2 * pair * LANES : (2 * pair + 1) * LANES]
        odd = out[:, (2 * pair + 1) * LANES : (2 * pair + 2) * LANES]
        at = pl.ds(pair * LANES, LANES)
        gate_ref[:, at] = jnp.where(first, even, pltpu.roll(odd, DH, 1)).astype(jnp.bfloat16)
        query = jnp.where(first, pltpu.roll(even, DH, 1), odd).astype(jnp.bfloat16)
        query_ref[:, at] = query * jnp.bfloat16(0.5 / DH**0.5)


def project(tokens, w_proj):
    rows, width = tokens.shape
    columns = w_proj.shape[1] // 2
    step = 256
    out = jax.ShapeDtypeStruct((rows, columns), jnp.bfloat16)
    return pl.pallas_call(
        proj_kernel,
        grid=(rows // step,),
        out_shape=(out, out),
        in_specs=[
            pl.BlockSpec((step, width), lambda i: (i, 0)),
            pl.BlockSpec(w_proj.shape, lambda i: (0, 0)),
        ],
        out_specs=[pl.BlockSpec((step, columns), lambda i: (i, 0))] * 2,
        compiler_params=pltpu.CompilerParams(vmem_limit_bytes=32 * 2**20),
        cost_estimate=pl.CostEstimate(
            flops=4 * rows * width * columns, bytes_accessed=4 * rows * width, transcendentals=0
        ),
    )(tokens, w_proj)


def attend_kernel(count_ref, slot_ref, live_ref, q_ref, kv_ref, out_ref, qp_ref, acc_ref):
    d = pl.program_id(0)
    n = count_ref[d]
    heads = q_ref.shape[2] // DH
    first = lax.broadcasted_iota(jnp.int32, (q_ref.shape[1], LANES), 1) < DH
    for pair in range(heads // 2):
        packed = q_ref[0, :, pair * LANES : (pair + 1) * LANES].astype(jnp.float32)
        even = jnp.where(first, packed, 0.0)
        odd = jnp.where(first, pltpu.roll(packed, DH, 1), 0.0)
        qp_ref[2 * pair] = even.astype(jnp.bfloat16)
        qp_ref[2 * pair + 1] = odd.astype(jnp.bfloat16)
    acc_ref[...] = jnp.zeros_like(acc_ref)
    event = lax.broadcasted_iota(jnp.int32, (BLK, LANES), 0)

    @pl.loop(0, (n + 1) // 2)
    def _(step):
        k0, k1 = slot_ref[d, 2 * step], slot_ref[d, 2 * step + 1]
        keep0 = (event < live_ref[d, 2 * step]).astype(jnp.float32).astype(jnp.bfloat16)
        keep1 = (event < live_ref[d, 2 * step + 1]).astype(jnp.float32).astype(jnp.bfloat16)
        for h in range(heads):
            at = slice(h * LANES, (h + 1) * LANES)
            kv = jnp.concatenate(
                [kv_ref[0, 0, k0, :, at] * keep0, kv_ref[0, 0, k1, :, at] * keep1], axis=0
            )
            half = lax.dot_general(
                qp_ref[h], kv, (((1,), (1,)), ((), ())), preferred_element_type=jnp.float32
            )
            weights = (half + half * jnp.tanh(half)).astype(jnp.bfloat16)
            acc_ref[h] += jnp.dot(weights, kv, preferred_element_type=jnp.float32)

    for pair in range(heads // 2):
        even, odd = acc_ref[2 * pair], acc_ref[2 * pair + 1]
        out_ref[0, :, pair * LANES : (pair + 1) * LANES] = jnp.where(
            first, pltpu.roll(even, DH, 1), odd
        ).astype(jnp.bfloat16)


def attend(count, slot, live, queries, kv_cache):
    scorers, rows, width = queries.shape
    heads = width // DH
    most = kv_cache.shape[2]
    flops = scorers * rows * most * BLK * width
    return pl.pallas_call(
        attend_kernel,
        grid_spec=pltpu.PrefetchScalarGridSpec(
            num_scalar_prefetch=3,
            grid=(scorers,),
            in_specs=[
                pl.BlockSpec((1, rows, width), lambda d, *_: (d, 0, 0)),
                pl.BlockSpec((1, 1) + kv_cache.shape[2:], lambda d, *_: (0, d, 0, 0, 0)),
            ],
            out_specs=pl.BlockSpec((1, rows, width), lambda d, *_: (d, 0, 0)),
            scratch_shapes=[
                pltpu.VMEM((heads, rows, LANES), jnp.bfloat16),
                pltpu.VMEM((heads, rows, LANES), jnp.float32),
            ],
        ),
        out_shape=jax.ShapeDtypeStruct(queries.shape, jnp.bfloat16),
        compiler_params=pltpu.CompilerParams(vmem_limit_bytes=40 * 2**20),
        cost_estimate=pl.CostEstimate(
            flops=8 * flops, bytes_accessed=kv_cache.size * 2, transcendentals=0
        ),
    )(count, slot, live, queries, kv_cache)


def tables(slot_request, lengths, block_owner, most, slots):
    total = lengths.shape[0]
    match = slot_request[:, None] == jnp.arange(total, dtype=jnp.int32)[None, :]
    slot_lengths = jnp.sum(jnp.where(match, lengths[None, :], 0), axis=1)
    starts = jnp.arange(MAXB, dtype=jnp.int32) * BLK
    live = jnp.clip(slot_lengths[:, None] - starts[None, :], 0, BLK).reshape(-1)
    both = lax.all_gather(jnp.stack([block_owner[:, 0], live]), "req", axis=0)
    owners, live = both[:, 0], both[:, 1]
    mine = owners == lax.axis_index("req")
    row = jnp.arange(owners.shape[1], dtype=jnp.int32)
    earlier = row[None, :] < row[:, None]
    rank = jnp.sum((mine[:, None, :] & earlier[None]).astype(jnp.int32), axis=2)
    used = mine & (live > 0)
    made = []
    wide = most + most % 2
    for slot in range(slots):
        here = used & (row // MAXB == slot)[None]
        place = jnp.sum((here[:, None, :] & earlier[None]).astype(jnp.int32), axis=2)
        hit = here[:, None, :] & (
            place[:, None, :] == jnp.arange(wide, dtype=jnp.int32)[None, :, None]
        )
        made.append(
            (
                jnp.sum(here.astype(jnp.int32), axis=1),
                jnp.sum(jnp.where(hit, rank[:, None, :], 0), axis=2),
                jnp.sum(jnp.where(hit, live[:, None, :], 0), axis=2),
            )
        )
    return made


def finish(attn, gate, w_out):
    wide = attn.astype(jnp.float32)
    mean = jnp.mean(wide, axis=-1, keepdims=True)
    square = jnp.mean(wide * wide, axis=-1, keepdims=True)
    hidden = (wide - mean) * lax.rsqrt(square - mean * mean + 1e-05) * gate.astype(jnp.float32)
    return jnp.dot(
        hidden.astype(jnp.bfloat16), w_out, preferred_element_type=jnp.float32
    ).astype(jnp.bfloat16)


def shards(tokens, w_proj, w_out, kv_cache, slot_request, lengths, block_owner):
    gathered = lax.all_gather(tokens, "head", axis=0, tiled=True)
    slots = gathered.shape[0] // CAND
    made = tables(slot_request, lengths, block_owner, kv_cache.shape[2], slots)
    gate, query = project(gathered, w_proj)
    sums = []
    for slot in range(slots):
        queries = lax.all_gather(query[slot * CAND : (slot + 1) * CAND], "req", axis=0)
        part = attend(*made[slot], queries, kv_cache)
        sums.append(lax.psum_scatter(part, "req", scatter_dimension=0, tiled=False))
    attn = jnp.concatenate(sums, axis=0)
    attn = lax.all_to_all(attn, "head", split_axis=0, concat_axis=1, tiled=True)
    gate = lax.all_to_all(gate, "head", split_axis=0, concat_axis=1, tiled=True)
    return finish(attn, gate, w_out)


def solution(mesh):
    return jax.shard_map(
        shards,
        mesh=mesh,
        in_specs=(
            P(("req", "head"), None),
            P(None, "head"),
            P(),
            P("req", None, None, None, "head"),
            P("req"),
            P(),
            P("req", None),
        ),
        out_specs=P(("req", "head"), None),
        check_vma=False,
    )
```

```python
import functools

import jax
import jax.numpy as jnp
from jax import lax
from jax.experimental import pallas as pl
from jax.experimental.pallas import tpu as pltpu
from jax.sharding import PartitionSpec as P

DH = 64
CAND = 512
BLK = 128
MAXB = 32
LANES = 2 * DH


def proj_kernel(x_ref, w_ref, gate_ref, query_ref):
    x = x_ref[...].astype(jnp.float32)
    mean = jnp.mean(x, axis=-1, keepdims=True)
    square = jnp.mean(x * x, axis=-1, keepdims=True)
    normed = ((x - mean) * lax.rsqrt(square - mean * mean + 1e-05)).astype(jnp.bfloat16)
    half = 0.5 * jnp.dot(normed, w_ref[...], preferred_element_type=jnp.float32)
    out = half + half * jnp.tanh(half)
    first = lax.broadcasted_iota(jnp.int32, (x.shape[0], LANES), 1) < DH
    for pair in range(w_ref.shape[1] // (2 * LANES)):
        even = out[:, 2 * pair * LANES : (2 * pair + 1) * LANES]
        odd = out[:, (2 * pair + 1) * LANES : (2 * pair + 2) * LANES]
        at = pl.ds(pair * LANES, LANES)
        gate_ref[:, at] = jnp.where(first, even, pltpu.roll(odd, DH, 1)).astype(jnp.bfloat16)
        query = jnp.where(first, pltpu.roll(even, DH, 1), odd).astype(jnp.bfloat16)
        query_ref[:, at] = query * jnp.bfloat16(0.5 / DH**0.5)


def project(tokens, w_proj):
    rows, width = tokens.shape
    columns = w_proj.shape[1] // 2
    step = 256
    out = jax.ShapeDtypeStruct((rows, columns), jnp.bfloat16)
    return pl.pallas_call(
        proj_kernel,
        grid=(rows // step,),
        out_shape=(out, out),
        in_specs=[
            pl.BlockSpec((step, width), lambda i: (i, 0)),
            pl.BlockSpec(w_proj.shape, lambda i: (0, 0)),
        ],
        out_specs=[pl.BlockSpec((step, columns), lambda i: (i, 0))] * 2,
        compiler_params=pltpu.CompilerParams(vmem_limit_bytes=32 * 2**20),
        cost_estimate=pl.CostEstimate(
            flops=4 * rows * width * columns, bytes_accessed=4 * rows * width, transcendentals=0
        ),
    )(tokens, w_proj)


def attend_kernel(count_ref, slot_ref, live_ref, q_ref, kv_ref, out_ref, qp_ref, acc_ref):
    d = pl.program_id(0) * pl.num_programs(1) + pl.program_id(1)
    n = count_ref[d]
    heads = q_ref.shape[2] // DH
    first = lax.broadcasted_iota(jnp.int32, (q_ref.shape[1], LANES), 1) < DH
    for pair in range(heads // 2):
        packed = q_ref[0, :, pair * LANES : (pair + 1) * LANES].astype(jnp.float32)
        even = jnp.where(first, packed, 0.0)
        odd = jnp.where(first, pltpu.roll(packed, DH, 1), 0.0)
        qp_ref[2 * pair] = even.astype(jnp.bfloat16)
        qp_ref[2 * pair + 1] = odd.astype(jnp.bfloat16)
    acc_ref[...] = jnp.zeros_like(acc_ref)
    event = lax.broadcasted_iota(jnp.int32, (BLK, LANES), 0)

    @pl.loop(0, (n + 1) // 2)
    def _(step):
        k0, k1 = slot_ref[d, 2 * step], slot_ref[d, 2 * step + 1]
        keep0 = (event < live_ref[d, 2 * step]).astype(jnp.float32).astype(jnp.bfloat16)
        keep1 = (event < live_ref[d, 2 * step + 1]).astype(jnp.float32).astype(jnp.bfloat16)
        for h in range(heads):
            at = slice(h * LANES, (h + 1) * LANES)
            kv = jnp.concatenate(
                [kv_ref[0, 0, k0, :, at] * keep0, kv_ref[0, 0, k1, :, at] * keep1], axis=0
            )
            half = lax.dot_general(
                qp_ref[h], kv, (((1,), (1,)), ((), ())), preferred_element_type=jnp.float32
            )
            weights = (half + half * jnp.tanh(half)).astype(jnp.bfloat16)
            acc_ref[h] += jnp.dot(weights, kv, preferred_element_type=jnp.float32)

    for pair in range(heads // 2):
        even, odd = acc_ref[2 * pair], acc_ref[2 * pair + 1]
        out_ref[0, :, pair * LANES : (pair + 1) * LANES] = jnp.where(
            first, pltpu.roll(even, DH, 1), odd
        ).astype(jnp.bfloat16)


def attend(count, slot, live, queries, kv_cache):
    scorers, rows, width = queries.shape
    heads = width // DH
    most = kv_cache.shape[2]
    flops = scorers * rows * most * BLK * width
    return pl.pallas_call(
        attend_kernel,
        grid_spec=pltpu.PrefetchScalarGridSpec(
            num_scalar_prefetch=3,
            grid=(scorers, rows // CAND),
            in_specs=[
                pl.BlockSpec((1, CAND, width), lambda d, s, *_: (d, s, 0)),
                pl.BlockSpec((1, 1) + kv_cache.shape[2:], lambda d, s, *_: (0, d, 0, 0, 0)),
            ],
            out_specs=pl.BlockSpec((1, CAND, width), lambda d, s, *_: (d, s, 0)),
            scratch_shapes=[
                pltpu.VMEM((heads, CAND, LANES), jnp.bfloat16),
                pltpu.VMEM((heads, CAND, LANES), jnp.float32),
            ],
        ),
        out_shape=jax.ShapeDtypeStruct(queries.shape, jnp.bfloat16),
        compiler_params=pltpu.CompilerParams(vmem_limit_bytes=40 * 2**20),
        cost_estimate=pl.CostEstimate(
            flops=8 * flops, bytes_accessed=kv_cache.size * 2, transcendentals=0
        ),
    )(count, slot, live, queries, kv_cache)


def local_table(slot_request, lengths, block_owner):
    total = lengths.shape[0]
    match = slot_request[:, None] == jnp.arange(total, dtype=jnp.int32)[None, :]
    slot_lengths = jnp.sum(jnp.where(match, lengths[None, :], 0), axis=1)
    starts = jnp.arange(MAXB, dtype=jnp.int32) * BLK
    live = jnp.clip(slot_lengths[:, None] - starts[None, :], 0, BLK).reshape(-1)
    both = jnp.stack([block_owner[:, 0], live])
    return jnp.pad(both, ((0, 6), (0, -both.shape[1] % 128)))


def tables(owners, live, most, slots):
    mine = owners == lax.axis_index("req")
    row = jnp.arange(owners.shape[1], dtype=jnp.int32)
    earlier = row[None, :] < row[:, None]
    rank = jnp.sum((mine[:, None, :] & earlier[None]).astype(jnp.int32), axis=2)
    used = mine & (live > 0)
    same = (row[None, :] // MAXB) == (row[:, None] // MAXB)
    place = jnp.sum((used[:, None, :] & (earlier & same)[None]).astype(jnp.int32), axis=2)
    wide = most + most % 2
    shape = (owners.shape[0], slots, MAXB)
    used, rank, place, live = (v.reshape(shape) for v in (used, rank, place, live))
    hit = used[:, :, None, :] & (
        place[:, :, None, :] == jnp.arange(wide, dtype=jnp.int32)[None, None, :, None]
    )
    count = jnp.sum(used.astype(jnp.int32), axis=2).reshape(-1)
    slot = jnp.sum(jnp.where(hit, rank[:, :, None, :], 0), axis=3).reshape(-1, wide)
    events = jnp.sum(jnp.where(hit, live[:, :, None, :], 0), axis=3).reshape(-1, wide)
    return count, slot, events


MESH = pl.DeviceIdType.MESH


def grid_of(count):
    inner = 8 if count >= 32 else 2
    return count // inner, inner


def place_of(axis, count):
    outer, inner = grid_of(count)
    me = lax.axis_index(axis)
    return me, me // inner, me % inner


def neighbours(axis, count):
    outer, inner = grid_of(count)
    me, a, b = place_of(axis, count)
    return [
        (a + 1 < outer, me + inner),
        (a > 0, me - inner),
        (b + 1 < inner, me + 1),
        (b > 0, me - 1),
    ]


def meet(pairs):
    barrier = pltpu.get_barrier_semaphore()
    total = jnp.int32(0)
    for axis, near in pairs:
        for there, index in near:

            @pl.when(there)
            def _(axis=axis, index=index):
                pl.semaphore_signal(barrier, inc=1, device_id={axis: index}, device_id_type=MESH)

            total = total + jnp.where(there, 1, 0).astype(jnp.int32)
    pl.semaphore_wait(barrier, total)


def gather_kernel(jobs, *refs):
    count = len(jobs)
    sources, outs, scratch = refs[:count], refs[count : 2 * count], refs[2 * count :]
    meet([(axis, neighbours(axis, size)) for axis, size in jobs])
    late = []
    waiting = []
    for job, (axis, size) in enumerate(jobs):
        source, out = sources[job], outs[job]
        send, recv, own = scratch[3 * job : 3 * job + 3]
        outer, inner = grid_of(size)
        me, a, b = place_of(axis, size)
        near = neighbours(axis, size)

        def copy(src, item, way, axis=axis, out=out, send=send, recv=recv, near=near):
            return pltpu.make_async_remote_copy(
                src_ref=src,
                dst_ref=out.at[item],
                send_sem=send.at[item, way],
                recv_sem=recv.at[item],
                device_id={axis: near[way][1]},
                device_id_type=MESH,
            )

        local = pltpu.make_async_copy(source, out.at[me], own)
        local.start()
        late.append((None, local))
        for way in range(4):
            made = copy(source, me, way)

            @pl.when(near[way][0])
            def _(made=made):
                made.start()

            late.append((near[way][0], made))
        offsets = [
            (da, db)
            for da in range(1 - outer, outer)
            for db in range(1 - inner, inner)
            if (da, db) != (0, 0)
        ]
        for da, db in sorted(offsets, key=lambda o: (abs(o[0]) + abs(o[1]), abs(o[1]), o)):
            there = (a + da >= 0) & (a + da < outer) & (b + db >= 0) & (b + db < inner)
            item = me + da * inner + db
            if db == 0:
                ways = [0 if da < 0 else 1, 2, 3]
            else:
                ways = [2 if db < 0 else 3]
            waiting.append((abs(da) + abs(db), there, item, ways, copy, out, near))
    for _, there, item, ways, copy, out, near in sorted(waiting, key=lambda w: w[0]):

        @pl.when(there)
        def _(item=item, copy=copy, out=out):
            copy(out.at[item], item, 0).wait_recv()

        for way in ways:
            made = copy(out.at[item], item, way)

            @pl.when(there & near[way][0])
            def _(made=made):
                made.start()

            late.append((there & near[way][0], made))
    for there, made in late:
        if there is None:
            made.wait()
        else:

            @pl.when(there)
            def _(made=made):
                made.wait_send()


def gather(arrays, axes, collective_id):
    jobs = [(axis, lax.axis_size(axis)) for axis in axes]
    scratch = []
    for _, size in jobs:
        scratch += [
            pltpu.SemaphoreType.DMA((size, 4)),
            pltpu.SemaphoreType.DMA((size,)),
            pltpu.SemaphoreType.DMA,
        ]
    return pl.pallas_call(
        functools.partial(gather_kernel, jobs),
        out_shape=[
            jax.ShapeDtypeStruct((size,) + x.shape, x.dtype)
            for x, (_, size) in zip(arrays, jobs)
        ],
        in_specs=[pl.BlockSpec(memory_space=pl.ANY)] * len(jobs),
        out_specs=[pl.BlockSpec(memory_space=pl.ANY)] * len(jobs),
        scratch_shapes=scratch,
        compiler_params=pltpu.CompilerParams(collective_id=collective_id, has_side_effects=True),
    )(*arrays)


def sum_kernel(
    size, heads, part, gate, attn_out, gate_out, work, side, line, acc,
    side_send, side_recv, line_send, line_recv, head_send, head_recv, own_sem,
):
    outer, inner = grid_of(size)
    me, a, b = place_of("req", size)
    near = neighbours("req", size)
    head = lax.axis_index("head")
    peers = [(jnp.bool_(True), lax.rem(head + off, heads)) for off in range(1, heads)]
    meet([("req", near), ("head", peers)])
    quarter = gate.shape[0] // heads
    late = []

    def to_peers(source, out, kind):
        own = pltpu.make_async_copy(
            source.at[pl.ds(head * quarter, quarter)], out.at[head], own_sem.at[kind]
        )
        own.start()
        for _, peer in peers:
            made = pltpu.make_async_remote_copy(
                src_ref=source.at[pl.ds(peer * quarter, quarter)],
                dst_ref=out.at[head],
                send_sem=head_send.at[kind, peer],
                recv_sem=head_recv.at[kind, head],
                device_id={"head": peer},
                device_id_type=MESH,
            )
            made.start()
            late.append((None, made))
        return own

    def hop(source, way, item, buffer, send, recv, slot):
        return pltpu.make_async_remote_copy(
            src_ref=source,
            dst_ref=buffer.at[way % 2, slot],
            send_sem=send.at[way % 2, slot],
            recv_sem=recv.at[way % 2, slot],
            device_id={"req": near[way][1]},
            device_id_type=MESH,
        )

    def arrived(there, way, item, buffer, send, recv, slot):
        @pl.when(there)
        def _():
            hop(work.at[item], way, item, buffer, send, recv, slot).wait_recv()
            acc[...] += buffer[way % 2, slot].astype(jnp.float32)

    sides = (side, side_send, side_recv)
    lines = (line, line_send, line_recv)
    own_gate = to_peers(gate, gate_out, 0)
    order = sorted(range(1 - outer, outer), key=lambda da: (-abs(da), da))
    for far in range(inner - 1, 0, -1):
        for da in order:
            for way, db in ((2, far), (3, -far)):
                item = me + da * inner + db
                there = (a + da >= 0) & (a + da < outer) & (b + db >= 0) & (b + db < inner)
                fed = near[5 - way][0]
                if inner > 2:

                    @pl.when(there & fed)
                    def _(item=item, way=way):
                        acc[...] = part[item].astype(jnp.float32)
                        arrived(True, way, item, *sides, item)
                        work[item] = acc[...].astype(jnp.bfloat16)
                        hop(work.at[item], way, item, *sides, item).start()

                    ends = there & jnp.logical_not(fed)
                else:
                    ends = there
                made = hop(part.at[item], way, item, *sides, item)

                @pl.when(ends)
                def _(made=made):
                    made.start()

                late.append((there, made))
    for da in order:
        item = me + da * inner
        there = (a + da >= 0) & (a + da < outer)

        @pl.when(there)
        def _(da=da, item=item):
            acc[...] = part[item].astype(jnp.float32)
            for way in (2, 3):
                arrived(near[5 - way][0], way, item, *sides, item)
            for way in (0, 1):
                if (way == 0 and da >= 0) or (way == 1 and da <= 0):
                    arrived(near[1 - way][0], way, item, *lines, a + da)
            work[item] = acc[...].astype(jnp.bfloat16)
            if da:
                way = 0 if da > 0 else 1
                hop(work.at[item], way, item, *lines, a + da).start()

        if da:
            way = 0 if da > 0 else 1
            late.append((there, hop(work.at[item], way, item, *lines, a + da)))
    own_attn = to_peers(work.at[me], attn_out, 1)
    for kind, out in ((0, gate_out), (1, attn_out)):
        for _, peer in peers:
            pltpu.make_async_remote_copy(
                src_ref=out.at[peer],
                dst_ref=out.at[peer],
                send_sem=head_send.at[kind, peer],
                recv_sem=head_recv.at[kind, peer],
                device_id={"head": peer},
                device_id_type=MESH,
            ).wait_recv()
    own_gate.wait()
    own_attn.wait()
    for there, made in late:
        if there is None:
            made.wait_send()
        else:

            @pl.when(there)
            def _(made=made):
                made.wait_send()


def sum_over_owners(part, gate, collective_id):
    size, rows, width = part.shape
    heads = lax.axis_size("head")
    outer, _ = grid_of(size)
    out = jax.ShapeDtypeStruct((heads, rows // heads, width), jnp.bfloat16)
    return pl.pallas_call(
        functools.partial(sum_kernel, size, heads),
        out_shape=(out, out),
        in_specs=[pl.BlockSpec(memory_space=pltpu.VMEM)] * 2,
        out_specs=[pl.BlockSpec(memory_space=pltpu.VMEM)] * 2,
        scratch_shapes=[
            pltpu.VMEM((size, rows, width), jnp.bfloat16),
            pltpu.VMEM((2, size, rows, width), jnp.bfloat16),
            pltpu.VMEM((2, outer, rows, width), jnp.bfloat16),
            pltpu.VMEM((rows, width), jnp.float32),
            pltpu.SemaphoreType.DMA((2, size)),
            pltpu.SemaphoreType.DMA((2, size)),
            pltpu.SemaphoreType.DMA((2, outer)),
            pltpu.SemaphoreType.DMA((2, outer)),
            pltpu.SemaphoreType.DMA((2, heads)),
            pltpu.SemaphoreType.DMA((2, heads)),
            pltpu.SemaphoreType.DMA((2,)),
        ],
        compiler_params=pltpu.CompilerParams(
            collective_id=collective_id, has_side_effects=True, vmem_limit_bytes=56 * 2**20
        ),
    )(part, gate)


def finish(attn, gate, w_out):
    wide = attn.astype(jnp.float32)
    mean = jnp.mean(wide, axis=-1, keepdims=True)
    square = jnp.mean(wide * wide, axis=-1, keepdims=True)
    hidden = (wide - mean) * lax.rsqrt(square - mean * mean + 1e-05) * gate.astype(jnp.float32)
    return jnp.dot(
        hidden.astype(jnp.bfloat16), w_out, preferred_element_type=jnp.float32
    ).astype(jnp.bfloat16)


def shards(tokens, w_proj, w_out, kv_cache, slot_request, lengths, block_owner):
    blocks = block_owner.shape[0]
    gathered, table = gather(
        [tokens, local_table(slot_request, lengths, block_owner)], ["head", "req"], 0
    )
    gathered = gathered.reshape(-1, tokens.shape[1])
    slots = gathered.shape[0] // CAND
    made = tables(table[:, 0, :blocks], table[:, 1, :blocks], kv_cache.shape[2], slots)
    gate, query = project(gathered, w_proj)
    [queries] = gather([query], ["req"], 1)
    part = attend(*made, queries, kv_cache)
    attn, gate = sum_over_owners(part, gate, 2)
    attn, gate = (v.transpose(1, 0, 2).reshape(v.shape[1], -1) for v in (attn, gate))
    return finish(attn, gate, w_out)


def solution(mesh):
    return jax.shard_map(
        shards,
        mesh=mesh,
        in_specs=(
            P(("req", "head"), None),
            P(None, "head"),
            P(),
            P("req", None, None, None, "head"),
            P("req"),
            P(),
            P("req", None),
        ),
        out_specs=P(("req", "head"), None),
        check_vma=False,
    )
```

```python
import functools

import jax
import jax.numpy as jnp
from jax import lax
from jax.experimental import pallas as pl
from jax.experimental.pallas import tpu as pltpu
from jax.sharding import PartitionSpec as P

DH = 64
CAND = 512
BLK = 128
MAXB = 32
LANES = 2 * DH


def proj_kernel(x_ref, w_ref, gate_ref, query_ref):
    x = x_ref[...].astype(jnp.float32)
    mean = jnp.mean(x, axis=-1, keepdims=True)
    square = jnp.mean(x * x, axis=-1, keepdims=True)
    normed = ((x - mean) * lax.rsqrt(square - mean * mean + 1e-05)).astype(jnp.bfloat16)
    half = 0.5 * jnp.dot(normed, w_ref[...], preferred_element_type=jnp.float32)
    out = half + half * jnp.tanh(half)
    first = lax.broadcasted_iota(jnp.int32, (x.shape[0], LANES), 1) < DH
    for pair in range(w_ref.shape[1] // (2 * LANES)):
        even = out[:, 2 * pair * LANES : (2 * pair + 1) * LANES]
        odd = out[:, (2 * pair + 1) * LANES : (2 * pair + 2) * LANES]
        at = pl.ds(pair * LANES, LANES)
        gate_ref[:, at] = jnp.where(first, even, pltpu.roll(odd, DH, 1)).astype(jnp.bfloat16)
        query = jnp.where(first, pltpu.roll(even, DH, 1), odd).astype(jnp.bfloat16)
        query_ref[:, at] = query * jnp.bfloat16(0.5 / DH**0.5)


def project(tokens, w_proj):
    rows, width = tokens.shape
    columns = w_proj.shape[1] // 2
    step = 256
    out = jax.ShapeDtypeStruct((rows, columns), jnp.bfloat16)
    return pl.pallas_call(
        proj_kernel,
        grid=(rows // step,),
        out_shape=(out, out),
        in_specs=[
            pl.BlockSpec((step, width), lambda i: (i, 0)),
            pl.BlockSpec(w_proj.shape, lambda i: (0, 0)),
        ],
        out_specs=[pl.BlockSpec((step, columns), lambda i: (i, 0))] * 2,
        compiler_params=pltpu.CompilerParams(vmem_limit_bytes=32 * 2**20),
        cost_estimate=pl.CostEstimate(
            flops=4 * rows * width * columns, bytes_accessed=4 * rows * width, transcendentals=0
        ),
    )(tokens, w_proj)


def attend_kernel(count_ref, slot_ref, live_ref, q_ref, kv_ref, out_ref, qp_ref, acc_ref):
    d = pl.program_id(0) * pl.num_programs(1) + pl.program_id(1)
    n = count_ref[d]
    heads = q_ref.shape[2] // DH
    first = lax.broadcasted_iota(jnp.int32, (q_ref.shape[1], LANES), 1) < DH
    for pair in range(heads // 2):
        packed = q_ref[0, :, pair * LANES : (pair + 1) * LANES].astype(jnp.float32)
        even = jnp.where(first, packed, 0.0)
        odd = jnp.where(first, pltpu.roll(packed, DH, 1), 0.0)
        qp_ref[2 * pair] = even.astype(jnp.bfloat16)
        qp_ref[2 * pair + 1] = odd.astype(jnp.bfloat16)
    acc_ref[...] = jnp.zeros_like(acc_ref)
    event = lax.broadcasted_iota(jnp.int32, (BLK, LANES), 0)

    @pl.loop(0, (n + 1) // 2)
    def _(step):
        k0, k1 = slot_ref[d, 2 * step], slot_ref[d, 2 * step + 1]
        keep0 = (event < live_ref[d, 2 * step]).astype(jnp.float32).astype(jnp.bfloat16)
        keep1 = (event < live_ref[d, 2 * step + 1]).astype(jnp.float32).astype(jnp.bfloat16)
        for h in range(heads):
            at = slice(h * LANES, (h + 1) * LANES)
            kv = jnp.concatenate(
                [kv_ref[0, 0, k0, :, at] * keep0, kv_ref[0, 0, k1, :, at] * keep1], axis=0
            )
            half = lax.dot_general(
                qp_ref[h], kv, (((1,), (1,)), ((), ())), preferred_element_type=jnp.float32
            )
            weights = (half + half * jnp.tanh(half)).astype(jnp.bfloat16)
            acc_ref[h] += jnp.dot(weights, kv, preferred_element_type=jnp.float32)

    for pair in range(heads // 2):
        even, odd = acc_ref[2 * pair], acc_ref[2 * pair + 1]
        out_ref[0, :, pair * LANES : (pair + 1) * LANES] = jnp.where(
            first, pltpu.roll(even, DH, 1), odd
        ).astype(jnp.bfloat16)


def attend(count, slot, live, queries, kv_cache):
    scorers, rows, width = queries.shape
    heads = width // DH
    most = kv_cache.shape[2]
    flops = scorers * rows * most * BLK * width
    return pl.pallas_call(
        attend_kernel,
        grid_spec=pltpu.PrefetchScalarGridSpec(
            num_scalar_prefetch=3,
            grid=(scorers, rows // CAND),
            in_specs=[
                pl.BlockSpec((1, CAND, width), lambda d, s, *_: (d, s, 0)),
                pl.BlockSpec((1, 1) + kv_cache.shape[2:], lambda d, s, *_: (0, d, 0, 0, 0)),
            ],
            out_specs=pl.BlockSpec((1, CAND, width), lambda d, s, *_: (d, s, 0)),
            scratch_shapes=[
                pltpu.VMEM((heads, CAND, LANES), jnp.bfloat16),
                pltpu.VMEM((heads, CAND, LANES), jnp.float32),
            ],
        ),
        out_shape=jax.ShapeDtypeStruct(queries.shape, jnp.bfloat16),
        compiler_params=pltpu.CompilerParams(vmem_limit_bytes=40 * 2**20),
        cost_estimate=pl.CostEstimate(
            flops=8 * flops, bytes_accessed=kv_cache.size * 2, transcendentals=0
        ),
    )(count, slot, live, queries, kv_cache)


def local_table(slot_request, lengths, block_owner):
    total = lengths.shape[0]
    match = slot_request[:, None] == jnp.arange(total, dtype=jnp.int32)[None, :]
    slot_lengths = jnp.sum(jnp.where(match, lengths[None, :], 0), axis=1)
    starts = jnp.arange(MAXB, dtype=jnp.int32) * BLK
    live = jnp.clip(slot_lengths[:, None] - starts[None, :], 0, BLK).reshape(-1)
    both = jnp.stack([block_owner[:, 0], live])
    return jnp.pad(both, ((0, 6), (0, -both.shape[1] % 128)))


def tables(owners, live, most, slots):
    mine = owners == lax.axis_index("req")
    row = jnp.arange(owners.shape[1], dtype=jnp.int32)
    earlier = row[None, :] < row[:, None]
    rank = jnp.sum((mine[:, None, :] & earlier[None]).astype(jnp.int32), axis=2)
    used = mine & (live > 0)
    same = (row[None, :] // MAXB) == (row[:, None] // MAXB)
    place = jnp.sum((used[:, None, :] & (earlier & same)[None]).astype(jnp.int32), axis=2)
    wide = most + most % 2
    shape = (owners.shape[0], slots, MAXB)
    used, rank, place, live = (v.reshape(shape) for v in (used, rank, place, live))
    hit = used[:, :, None, :] & (
        place[:, :, None, :] == jnp.arange(wide, dtype=jnp.int32)[None, None, :, None]
    )
    count = jnp.sum(used.astype(jnp.int32), axis=2).reshape(-1)
    slot = jnp.sum(jnp.where(hit, rank[:, :, None, :], 0), axis=3).reshape(-1, wide)
    events = jnp.sum(jnp.where(hit, live[:, :, None, :], 0), axis=3).reshape(-1, wide)
    return count, slot, events


MESH = pl.DeviceIdType.MESH


def grid_of(count):
    inner = 8 if count >= 32 else 2
    return count // inner, inner


def place_of(axis, count):
    outer, inner = grid_of(count)
    me = lax.axis_index(axis)
    return me, me // inner, me % inner


def neighbours(axis, count):
    outer, inner = grid_of(count)
    me, a, b = place_of(axis, count)
    return [
        (a + 1 < outer, me + inner),
        (a > 0, me - inner),
        (b + 1 < inner, me + 1),
        (b > 0, me - 1),
    ]


def meet(pairs):
    barrier = pltpu.get_barrier_semaphore()
    total = jnp.int32(0)
    for axis, near in pairs:
        for there, index in near:

            @pl.when(there)
            def _(axis=axis, index=index):
                pl.semaphore_signal(barrier, inc=1, device_id={axis: index}, device_id_type=MESH)

            total = total + jnp.where(there, 1, 0).astype(jnp.int32)
    pl.semaphore_wait(barrier, total)


def gather_kernel(jobs, *refs):
    count = len(jobs)
    sources, outs, scratch = refs[:count], refs[count : 2 * count], refs[2 * count :]
    meet([(axis, neighbours(axis, size)) for axis, size in jobs])
    late = []
    waiting = []
    for job, (axis, size) in enumerate(jobs):
        source, out = sources[job], outs[job]
        send, recv, own = scratch[3 * job : 3 * job + 3]
        outer, inner = grid_of(size)
        me, a, b = place_of(axis, size)
        near = neighbours(axis, size)

        def copy(src, item, way, axis=axis, out=out, send=send, recv=recv, near=near):
            return pltpu.make_async_remote_copy(
                src_ref=src,
                dst_ref=out.at[item],
                send_sem=send.at[item, way],
                recv_sem=recv.at[item],
                device_id={axis: near[way][1]},
                device_id_type=MESH,
            )

        local = pltpu.make_async_copy(source, out.at[me], own)
        local.start()
        late.append((None, local))
        for way in range(4):
            made = copy(source, me, way)

            @pl.when(near[way][0])
            def _(made=made):
                made.start()

            late.append((near[way][0], made))
        offsets = [
            (da, db)
            for da in range(1 - outer, outer)
            for db in range(1 - inner, inner)
            if (da, db) != (0, 0)
        ]
        for da, db in sorted(offsets, key=lambda o: (abs(o[0]) + abs(o[1]), abs(o[1]), o)):
            there = (a + da >= 0) & (a + da < outer) & (b + db >= 0) & (b + db < inner)
            item = me + da * inner + db
            if db == 0:
                ways = [0 if da < 0 else 1, 2, 3]
            else:
                ways = [2 if db < 0 else 3]
            waiting.append((abs(da) + abs(db), there, item, ways, copy, out, near))
    for _, there, item, ways, copy, out, near in sorted(waiting, key=lambda w: w[0]):

        @pl.when(there)
        def _(item=item, copy=copy, out=out):
            copy(out.at[item], item, 0).wait_recv()

        for way in ways:
            made = copy(out.at[item], item, way)

            @pl.when(there & near[way][0])
            def _(made=made):
                made.start()

            late.append((there & near[way][0], made))
    for there, made in late:
        if there is None:
            made.wait()
        else:

            @pl.when(there)
            def _(made=made):
                made.wait_send()


def gather(arrays, axes, collective_id):
    jobs = [(axis, lax.axis_size(axis)) for axis in axes]
    scratch = []
    for _, size in jobs:
        scratch += [
            pltpu.SemaphoreType.DMA((size, 4)),
            pltpu.SemaphoreType.DMA((size,)),
            pltpu.SemaphoreType.DMA,
        ]
    return pl.pallas_call(
        functools.partial(gather_kernel, jobs),
        out_shape=[
            jax.ShapeDtypeStruct((size,) + x.shape, x.dtype)
            for x, (_, size) in zip(arrays, jobs)
        ],
        in_specs=[pl.BlockSpec(memory_space=pl.ANY)] * len(jobs),
        out_specs=[pl.BlockSpec(memory_space=pl.ANY)] * len(jobs),
        scratch_shapes=scratch,
        compiler_params=pltpu.CompilerParams(collective_id=collective_id, has_side_effects=True),
    )(*arrays)


def chunks_of(size):
    return 4 if grid_of(size)[1] == 2 else 1


def sum_kernel(
    size, heads, part, gate, attn_out, gate_out, work, side, line, acc,
    side_send, side_recv, line_send, line_recv, head_send, head_recv, own_sem,
):
    outer, inner = grid_of(size)
    me, a, b = place_of("req", size)
    near = neighbours("req", size)
    head = lax.axis_index("head")
    peers = [(jnp.bool_(True), lax.rem(head + off, heads)) for off in range(1, heads)]
    meet([("req", near), ("head", peers)])
    quarter = gate.shape[0] // heads
    chunks = chunks_of(size)
    rows = gate.shape[0] // chunks
    late = []

    def to_peer(source, out, kind, peer):
        rows_of = source.at[pl.ds(peer * quarter, quarter)]
        local = pltpu.make_async_copy(rows_of, out.at[head], own_sem.at[kind])
        made = pltpu.make_async_remote_copy(
            src_ref=rows_of,
            dst_ref=out.at[head],
            send_sem=head_send.at[kind, peer],
            recv_sem=head_recv.at[kind, head],
            device_id={"head": jnp.int32(peer)},
            device_id_type=MESH,
        )

        @pl.when(head == peer)
        def _():
            local.start()

        @pl.when(head != peer)
        def _():
            made.start()

        owned.append((head == peer, local))
        late.append((head != peer, made))

    def hop(source, way, item, chunk, buffer, send, recv, slot):
        return pltpu.make_async_remote_copy(
            src_ref=source.at[item, pl.ds(chunk * rows, rows)],
            dst_ref=buffer.at[way % 2, slot, pl.ds(chunk * rows, rows)],
            send_sem=send.at[way % 2, slot * chunks + chunk],
            recv_sem=recv.at[way % 2, slot * chunks + chunk],
            device_id={"req": near[way][1]},
            device_id_type=MESH,
        )

    def arrived(there, way, item, chunk, buffer, send, recv, slot):
        @pl.when(there)
        def _():
            hop(work, way, item, chunk, buffer, send, recv, slot).wait_recv()
            acc[...] += buffer[way % 2, slot, chunk * rows : (chunk + 1) * rows].astype(jnp.float32)

    owned = []
    sides = (side, side_send, side_recv)
    lines = (line, line_send, line_recv)
    order = sorted(range(1 - outer, outer), key=lambda da: (-abs(da), da))
    for far in range(inner - 1, 0, -1):
        for da, chunk in [(da, chunk) for da in order for chunk in range(chunks)]:
            at = slice(chunk * rows, (chunk + 1) * rows)
            for way, db in ((2, far), (3, -far)):
                item = me + da * inner + db
                there = (a + da >= 0) & (a + da < outer) & (b + db >= 0) & (b + db < inner)
                fed = near[5 - way][0]
                if inner > 2:

                    @pl.when(there & fed)
                    def _(item=item, way=way, chunk=chunk, at=at):
                        acc[...] = part[item, at].astype(jnp.float32)
                        arrived(True, way, item, chunk, *sides, item)
                        work[item, at] = acc[...].astype(jnp.bfloat16)
                        hop(work, way, item, chunk, *sides, item).start()

                    ends = there & jnp.logical_not(fed)
                else:
                    ends = there
                made = hop(part, way, item, chunk, *sides, item)

                @pl.when(ends)
                def _(made=made):
                    made.start()

                late.append((there, made))
    for peer in range(heads):
        to_peer(gate, gate_out, 0, peer)
    for da, chunk in [(da, chunk) for da in order for chunk in range(chunks)]:
        at = slice(chunk * rows, (chunk + 1) * rows)
        item = me + da * inner
        there = (a + da >= 0) & (a + da < outer)

        @pl.when(there)
        def _(da=da, item=item, chunk=chunk, at=at):
            acc[...] = part[item, at].astype(jnp.float32)
            for way in (2, 3):
                arrived(near[5 - way][0], way, item, chunk, *sides, item)
            for way in (0, 1):
                if (way == 0 and da >= 0) or (way == 1 and da <= 0):
                    arrived(near[1 - way][0], way, item, chunk, *lines, a + da)
            work[item, at] = acc[...].astype(jnp.bfloat16)
            if da:
                hop(work, 0 if da > 0 else 1, item, chunk, *lines, a + da).start()

        if da:
            late.append((there, hop(work, 0 if da > 0 else 1, item, chunk, *lines, a + da)))
        else:
            for peer in range(chunk * heads // chunks, (chunk + 1) * heads // chunks):
                to_peer(work.at[me], attn_out, 1, peer)
    for kind, out in ((0, gate_out), (1, attn_out)):
        for _, peer in peers:
            pltpu.make_async_remote_copy(
                src_ref=out.at[peer],
                dst_ref=out.at[peer],
                send_sem=head_send.at[kind, peer],
                recv_sem=head_recv.at[kind, peer],
                device_id={"head": peer},
                device_id_type=MESH,
            ).wait_recv()
    for there, made in owned:

        @pl.when(there)
        def _(made=made):
            made.wait()

    for there, made in late:

        @pl.when(there)
        def _(made=made):
            made.wait_send()


def sum_over_owners(part, gate, collective_id):
    size, rows, width = part.shape
    heads = lax.axis_size("head")
    outer, _ = grid_of(size)
    chunks = chunks_of(size)
    out = jax.ShapeDtypeStruct((heads, rows // heads, width), jnp.bfloat16)
    return pl.pallas_call(
        functools.partial(sum_kernel, size, heads),
        out_shape=(out, out),
        in_specs=[pl.BlockSpec(memory_space=pltpu.VMEM)] * 2,
        out_specs=[pl.BlockSpec(memory_space=pltpu.VMEM)] * 2,
        scratch_shapes=[
            pltpu.VMEM((size, rows, width), jnp.bfloat16),
            pltpu.VMEM((2, size, rows, width), jnp.bfloat16),
            pltpu.VMEM((2, outer, rows, width), jnp.bfloat16),
            pltpu.VMEM((rows // chunks, width), jnp.float32),
            pltpu.SemaphoreType.DMA((2, size * chunks)),
            pltpu.SemaphoreType.DMA((2, size * chunks)),
            pltpu.SemaphoreType.DMA((2, outer * chunks)),
            pltpu.SemaphoreType.DMA((2, outer * chunks)),
            pltpu.SemaphoreType.DMA((2, heads)),
            pltpu.SemaphoreType.DMA((2, heads)),
            pltpu.SemaphoreType.DMA((2,)),
        ],
        compiler_params=pltpu.CompilerParams(
            collective_id=collective_id, has_side_effects=True, vmem_limit_bytes=56 * 2**20
        ),
    )(part, gate)


def finish_kernel(attn_ref, gate_ref, w_ref, out_ref):
    parts, _, width = attn_ref.shape
    wide = [attn_ref[i].astype(jnp.float32) for i in range(parts)]
    mean = sum(jnp.sum(v, axis=-1, keepdims=True) for v in wide) / (parts * width)
    square = sum(jnp.sum(v * v, axis=-1, keepdims=True) for v in wide) / (parts * width)
    scale = lax.rsqrt(square - mean * mean + 1e-05)
    hidden = jnp.concatenate(
        [
            ((wide[i] - mean) * scale * gate_ref[i].astype(jnp.float32)).astype(jnp.bfloat16)
            for i in range(parts)
        ],
        axis=1,
    )
    out_ref[...] = jnp.dot(hidden, w_ref[...], preferred_element_type=jnp.float32).astype(
        jnp.bfloat16
    )


def finish(attn, gate, w_out):
    parts, rows, width = attn.shape
    columns = w_out.shape[1]
    step = 512
    return pl.pallas_call(
        finish_kernel,
        grid=(columns // step,),
        out_shape=jax.ShapeDtypeStruct((rows, columns), jnp.bfloat16),
        in_specs=[
            pl.BlockSpec(attn.shape, lambda i: (0, 0, 0)),
            pl.BlockSpec(gate.shape, lambda i: (0, 0, 0)),
            pl.BlockSpec((w_out.shape[0], step), lambda i: (0, i)),
        ],
        out_specs=pl.BlockSpec((rows, step), lambda i: (0, i)),
        compiler_params=pltpu.CompilerParams(vmem_limit_bytes=32 * 2**20),
    )(attn, gate, w_out)


def shards(tokens, w_proj, w_out, kv_cache, slot_request, lengths, block_owner):
    blocks = block_owner.shape[0]
    gathered, table = gather(
        [tokens, local_table(slot_request, lengths, block_owner)], ["head", "req"], 0
    )
    gathered = gathered.reshape(-1, tokens.shape[1])
    slots = gathered.shape[0] // CAND
    made = tables(table[:, 0, :blocks], table[:, 1, :blocks], kv_cache.shape[2], slots)
    gate, query = project(gathered, w_proj)
    [queries] = gather([query], ["req"], 1)
    part = attend(*made, queries, kv_cache)
    attn, gate = sum_over_owners(part, gate, 2)
    return finish(attn, gate, w_out)


def solution(mesh):
    return jax.shard_map(
        shards,
        mesh=mesh,
        in_specs=(
            P(("req", "head"), None),
            P(None, "head"),
            P(),
            P("req", None, None, None, "head"),
            P("req"),
            P(),
            P("req", None),
        ),
        out_specs=P(("req", "head"), None),
        check_vma=False,
    )
```
